512 devices in a mesh: dp: 32 (over x, y), tensor: 16 (over z, core).
Axes of the slice: x: 4, y: 8, z: 8, core: 2. Of those that a mesh axis runs over, the one named last changes fastest.
Arguments:
- grad: bfloat16 [4096, 28672], P('tensor', 'dp'), may hold values from -6 to 6
- error: float32 [4096, 28672], P('tensor', 'dp'), may hold values from -4 to 4
- q_start: bfloat16 [14336, 64], replicated, may hold values from -0.046875 to 0.046875
Outputs:
- new_error: float32 [4096, 28672], P('tensor', 'dp')
- q_new: float32 [14336, 64], P(('dp', 'tensor'))
The draws below stay inside these ranges and needn't reach their ends.
All inputs are finite; a program needn't handle non-finite values.
Results may differ from the reference program's by a relative error of at most 0.00045.
Values sent between devices are 32-bit elements; how exact they have to be, the bound alone decides.
No kernel may reach another device: no remote copies, remote signals or barrier semaphores. Data moves between devices by JAX's collectives and lax.ppermute only.
A program may use at most 64 MiB of HBM per device.

```python
import jax
import jax.numpy as jnp
from jax import lax

ROWS = 4096
COLS = 14336
RANK = 64
REPLICAS = 2


def with_spikes(result, own_key, source, target, blocks, factor):
    def block_of(position):
        return (jnp.arange(result.shape[position]) // (result.shape[position] // blocks)).reshape((-1,) + (1,) * (result.ndim - 1 - position))

    first = jax.random.permutation(own_key, blocks)[block_of(target)]
    far = (block_of(target) + blocks // 2) % blocks
    return jnp.where((block_of(source) == first) | (block_of(source) == far), factor * result, result)


def block_scale(rng, dims, cuts, least, high):
    loudness = 1.0
    for position, shards_of in cuts:
        heights = jax.random.uniform(jax.random.fold_in(jax.random.fold_in(rng, 6), position), (shards_of,), jnp.float32, least / len(cuts), high / len(cuts))
        loudness = loudness * jnp.repeat(jnp.exp(heights), dims[position] // shards_of).reshape((-1,) + (1,) * (len(dims) - 1 - position))
    return loudness


def scatter_about(stream_key, extent, scale, most, pieces=(), kind=jnp.bfloat16):
    entries = jax.random.normal(stream_key, extent, jnp.float32) * scale
    if len(pieces) > 0:
        entries = block_scale(stream_key, extent, pieces, -0.22, 0.18) * entries
    return jnp.clip(entries, min=-most, max=most).astype(kind)


def noise_with(rng, dims, width, bound, cuts, heavy, held_as=jnp.bfloat16):
    result = width * jax.random.normal(rng, dims, jnp.float32)
    if cuts:
        result = result * block_scale(rng, dims, cuts, -0.22, 0.18)
    return jnp.clip(with_spikes(result, jax.random.fold_in(rng, 3), *heavy), -bound, bound).astype(held_as)


def setup_inputs(seed: int = 0) -> dict:
    arg_keys = jax.random.split(jax.random.key(seed), 4)
    grad = noise_with(arg_keys[0], (ROWS, REPLICAS * COLS), 1.0, 6.0, ((0, 16), (1, 32)), (0, 1, 32, 2.75))
    error = scatter_about(arg_keys[1], (ROWS, REPLICAS * COLS), 0.5, 4.0, ((0, 16), (1, 32)), jnp.float32)
    q_start = scatter_about(arg_keys[2], (COLS, RANK), COLS ** -0.5, 0.046875)
    return dict(grad=grad, error=error, q_start=q_start)


def reference(grad, error, q_start):
    highest = lax.Precision.HIGHEST
    merged = grad.astype(jnp.float32) + error
    blocks = merged.reshape(ROWS, REPLICAS, COLS)
    q_input = q_start.astype(jnp.float32)
    p_mean = jnp.einsum('irj,jk->ik', blocks, q_input, precision=highest) / REPLICAS
    gram = jnp.dot(p_mean.T, p_mean, precision=highest)
    lower = jnp.linalg.cholesky(gram)
    basis = lax.linalg.triangular_solve(lower, p_mean, left_side=False, lower=True, transpose_a=True)
    q_new = jnp.einsum('irj,ik->jk', blocks, basis, precision=highest) / REPLICAS
    approx = jnp.dot(basis, q_new.T, precision=highest)
    new_error = (blocks - approx[:, None, :]).reshape(ROWS, REPLICAS * COLS)
    return (new_error, q_new)
```

```python
import jax
import jax.numpy as jnp
from jax import lax
from jax.experimental import pallas as pl
from jax.experimental.pallas import tpu as pltpu
from jax.sharding import Mesh, PartitionSpec as P

REPLICAS = 2
RANK = 64
PARTS = 32
OWN = 28
SLOT = 16
NT = (((1,), (1,)), ((), ()))
NN = (((1,), (0,)), ((), ()))
BF16 = jnp.bfloat16
F32 = jnp.float32


def split(value):
    high = value.astype(BF16)
    return high, (value - high.astype(F32)).astype(BF16)


def dot(a, b, dims):
    return lax.dot_general(a, b, dims, preferred_element_type=F32)


def dot3(a, b, dims):
    a_high, a_low = split(a)
    b_high, b_low = split(b)
    return dot(a_high, b_high, dims) + (dot(a_high, b_low, dims) + dot(a_low, b_high, dims))


def left_kernel(col_ref, grad_ref, error_ref, q_ref, out_ref):
    high, low = split(grad_ref[...].astype(F32) + error_ref[...])
    q = q_ref[...]
    p = dot(high, q, NN) + dot(low, q, NN)
    half = p.shape[0] // 2
    out_ref[...] = jnp.concatenate([p[:half], p[half:]], axis=1)


def arrange_kernel(grad_ref, error_ref, first_high_ref, first_low_ref, last_high_ref, last_low_ref):
    high, low = split(grad_ref[...].astype(F32) + error_ref[...])
    shape = (PARTS * SLOT, high.shape[1])
    row = lax.broadcasted_iota(jnp.int32, shape, 0)
    col = lax.broadcasted_iota(jnp.int32, shape, 1)
    within = row % SLOT
    place = OWN * (row // SLOT) + within
    first = (col == place).astype(F32).astype(BF16)
    last = ((col == place + SLOT) & (within < OWN - SLOT)).astype(F32).astype(BF16)
    first_high_ref[...] = dot(first, high, NT).astype(BF16)
    first_low_ref[...] = dot(first, low, NT).astype(BF16)
    last_high_ref[...] = dot(last, high, NT).astype(BF16)
    last_low_ref[...] = dot(last, low, NT).astype(BF16)


def sum_left_kernel(in_ref, out_ref):
    rows = in_ref.shape[0]
    total = jnp.sum(in_ref[...].reshape(rows // 8, 8, 128), axis=0)
    total = total + pltpu.roll(total, 4, 0)
    out_ref[...] = jnp.broadcast_to(total[None], (rows // 8, 8, 128)).reshape(rows, 128)


def right_kernel(p_ref, first_high_ref, first_low_ref, last_high_ref, last_low_ref, out_ref, gram_ref):
    top = p_ref[...]
    bottom = pltpu.roll(top, RANK, 1)
    lane = lax.broadcasted_iota(jnp.int32, top.shape, 1)
    lower = lane < RANK
    zero = jnp.zeros_like(top)
    left = jnp.concatenate([jnp.where(lower, top, zero), jnp.where(lower, bottom, zero)], axis=0)
    right = jnp.concatenate([jnp.where(lower, zero, bottom), jnp.where(lower, zero, top)], axis=0)
    left_high, left_low = split(left)
    right_high, right_low = split(right)
    left_both = jnp.concatenate([left_high, left_low], axis=1)
    right_both = jnp.concatenate([right_high, right_low], axis=1)
    both = (
        dot(first_high_ref[...], left_both, NN)
        + dot(last_high_ref[...], right_both, NN)
        + dot(first_low_ref[...], left_both, NN)
        + dot(last_low_ref[...], right_both, NN)
    )
    out_ref[...] = both[:, :128] + both[:, 128:]
    turned = top.T
    turned = jnp.concatenate([turned[:RANK], turned[RANK:]], axis=1)
    gram_ref[...] = dot3(turned, right, NN)
    for k in range(PARTS):
        out_ref[SLOT * k + 12 : SLOT * k + 14, RANK:] = gram_ref[2 * k : 2 * k + 2, RANK:]


def sum_right_kernel(in_ref, out_ref, own_ref):
    total = jnp.sum(in_ref[...].reshape(PARTS, SLOT, 128), axis=0)
    own_ref[...] = total
    out_ref[...] = jnp.broadcast_to(total[None], (PARTS, SLOT, 128)).reshape(PARTS * SLOT, 128)


def eliminate(tiles):
    sub = lax.broadcasted_iota(jnp.int32, (8, 128), 0)
    spread = lambda value: jnp.broadcast_to(value, (8, 128))
    scales = [jnp.zeros((8, 128), F32) for _ in tiles]
    count = len(tiles)
    width = 4
    for start in range(0, RANK, width):
        t = start // 8
        offset = start % 8
        cols = [
            {i: spread(tiles[i][:, RANK + start + q : RANK + start + q + 1]) for i in range(t, count)}
            for q in range(width)
        ]
        rows = [spread(tiles[t][offset + q : offset + q + 1, :]) for q in range(width)]
        for q in range(width):
            row = offset + q
            pivot = spread(cols[q][t][row : row + 1, :])
            inverse = 1.0 / pivot
            root = lax.rsqrt(pivot)
            root = root * (1.5 - 0.5 * pivot * root * root)
            scales[t] = jnp.where(sub == row, root, scales[t])
            scaled = rows[q] * inverse
            factor = dict(cols[q])
            factor[t] = jnp.where(sub > row, cols[q][t], 0.0)
            for q2 in range(q + 1, width):
                entry = spread(cols[q2][t][row : row + 1, :]) * inverse
                rows[q2] = rows[q2] - spread(factor[t][offset + q2 : offset + q2 + 1, :]) * scaled
                for i in range(t, count):
                    cols[q2][i] = cols[q2][i] - factor[i] * entry
            for i in range(t, count):
                tiles[i] = tiles[i] - factor[i] * scaled
    return [tile * scale for tile, scale in zip(tiles, scales)]


def error_kernel(grad_ref, error_ref, p_ref, s_ref, own_ref, error_out_ref, q_out_ref, table_ref, right_ref):
    row = lax.broadcasted_iota(jnp.int32, (RANK, 128), 0)
    lane = lax.broadcasted_iota(jnp.int32, (RANK, 128), 1)
    table_ref[...] = (row == lane).astype(F32)
    for k in range(PARTS):
        table_ref[2 * k : 2 * k + 2, RANK:] = 0.5 * s_ref[SLOT * k + 12 : SLOT * k + 14, RANK:]
    tiles = eliminate([table_ref[8 * i : 8 * i + 8, :] for i in range(RANK // 8)])
    inverse = jnp.where(lane < RANK, jnp.concatenate(tiles, axis=0), 0.0)
    both = jnp.concatenate([inverse, pltpu.roll(inverse, RANK, 1)], axis=0)
    basis = dot3(p_ref[...], both, NT)
    basis = jnp.concatenate([basis[:, :RANK], basis[:, RANK:]], axis=0)
    right = 0.5 * dot3(s_ref[...], both, NT)
    shifted = pltpu.roll(right, RANK, 1)
    for k in range(PARTS):
        right_ref[OWN * k : OWN * k + SLOT, :] = right[SLOT * k : SLOT * k + SLOT, :RANK]
        right_ref[OWN * k + SLOT : OWN * k + OWN, :] = shifted[SLOT * k : SLOT * k + OWN - SLOT, :RANK]
    own = 0.5 * dot3(own_ref[...], both, NT)
    q_out_ref[:SLOT, :] = own[:, :RANK]
    q_out_ref[SLOT:, :] = pltpu.roll(own, RANK, 1)[: OWN - SLOT, :RANK]
    merged = grad_ref[...].astype(F32) + error_ref[...]
    error_out_ref[...] = merged - dot3(basis, right_ref[...], NT)


def shape(*dims, kind=F32):
    return jax.ShapeDtypeStruct(dims, kind)


def params():
    return pltpu.CompilerParams(vmem_limit_bytes=24 * 1024 * 1024)


def shards(grad, error, q_start):
    rows, cols = grad.shape
    col = lax.axis_index("col").astype(jnp.int32).reshape(1)
    with jax.named_scope("left"):
        p_own = pl.pallas_call(
            left_kernel,
            grid_spec=pltpu.PrefetchScalarGridSpec(
                num_scalar_prefetch=1,
                grid=(1,),
                in_specs=[
                    pl.BlockSpec((rows, cols), lambda i, c: (0, 0)),
                    pl.BlockSpec((rows, cols), lambda i, c: (0, 0)),
                    pl.BlockSpec((cols, RANK), lambda i, c: (c[0], 0)),
                ],
                out_specs=pl.BlockSpec((rows // 2, 128), lambda i, c: (0, 0)),
            ),
            out_shape=shape(rows // 2, 128),
            compiler_params=params(),
        )(col, grad, error, q_start)
    with jax.named_scope("left_scatter"):
        p_parts = lax.all_to_all(p_own, ("rep", "col"), 0, 0, tiled=True)
    with jax.named_scope("arrange"):
        arranged = pl.pallas_call(
            arrange_kernel,
            out_shape=[shape(PARTS * SLOT, rows, kind=BF16)] * 4,
            compiler_params=params(),
            cost_estimate=pl.CostEstimate(flops=2 * 4 * 512 * 256 * 896, bytes_accessed=2500000, transcendentals=0),
        )(grad, error)
    with jax.named_scope("left_sum"):
        p_sum = pl.pallas_call(sum_left_kernel, out_shape=shape(rows // 2, 128), compiler_params=params())(p_parts)
    with jax.named_scope("left_gather"):
        p = lax.all_to_all(p_sum, ("rep", "col"), 0, 0, tiled=True)
    with jax.named_scope("right"):
        s_own = pl.pallas_call(
            right_kernel,
            out_shape=shape(PARTS * SLOT, 128),
            scratch_shapes=[pltpu.VMEM((RANK, 128), F32)],
            compiler_params=params(),
        )(p, *arranged)
    with jax.named_scope("right_scatter"):
        s_parts = lax.all_to_all(s_own, ("rep", "tensor"), 0, 0, tiled=True)
    with jax.named_scope("right_sum"):
        s_sum, s_piece = pl.pallas_call(
            sum_right_kernel,
            out_shape=[shape(PARTS * SLOT, 128), shape(SLOT, 128)],
            compiler_params=params(),
        )(s_parts)
    with jax.named_scope("right_owner"):
        own = lax.ppermute(
            s_piece, ("rep", "col"), [(s, REPLICAS * (s % 16) + s // 16) for s in range(PARTS)]
        )
    with jax.named_scope("right_gather"):
        s = lax.all_to_all(s_sum, ("rep", "tensor"), 0, 0, tiled=True)
    with jax.named_scope("new_error"):
        return pl.pallas_call(
            error_kernel,
            out_shape=[shape(rows, cols), shape(OWN, RANK)],
            scratch_shapes=[pltpu.VMEM((RANK, 128), F32), pltpu.VMEM((cols, RANK), F32)],
            compiler_params=params(),
        )(grad, error, p, s, own)


def solution(mesh):
    n_dp, n_tensor = mesh.devices.shape
    fine = Mesh(mesh.devices.reshape(REPLICAS, n_dp // REPLICAS, n_tensor), ("rep", "col", "tensor"))
    return jax.shard_map(
        shards,
        mesh=fine,
        in_specs=(P("tensor", ("rep", "col")), P("tensor", ("rep", "col")), P()),
        out_specs=(P("tensor", ("rep", "col")), P(("rep", "col", "tensor"), None)),
        check_vma=False,
    )
```

```python
import jax
import jax.numpy as jnp
from jax import lax
from jax.experimental import pallas as pl
from jax.experimental.pallas import tpu as pltpu
from jax.sharding import Mesh, PartitionSpec as P

REPLICAS = 2
RANK = 64
PARTS = 32
OWN = 28
CHUNKS = 4
LEFT_LIMIT = 62
WIDTH = 8
SLOT = 16
NT = (((1,), (1,)), ((), ()))
NN = (((1,), (0,)), ((), ()))
BF16 = jnp.bfloat16
F32 = jnp.float32


def split(value):
    high = value.astype(BF16)
    return high, (value - high.astype(F32)).astype(BF16)


def dot(a, b, dims):
    return lax.dot_general(a, b, dims, preferred_element_type=F32)


def dot3(a, b, dims):
    a_high, a_low = split(a)
    b_high, b_low = split(b)
    return dot(a_high, b_high, dims) + (dot(a_high, b_low, dims) + dot(a_low, b_high, dims))


def left_kernel(col_ref, grad_ref, error_ref, q_ref, out_ref, grad_own, error_own, q_own, sems):
    rows, cols = grad_own.shape
    step = rows // CHUNKS
    start = pl.multiple_of(col_ref[0] * cols, 128)
    q_copy = pltpu.make_async_copy(q_ref.at[:, pl.ds(start, cols)], q_own, sems.at[0])
    q_copy.start()
    copies = []
    for i in range(CHUNKS):
        part = pl.ds(i * step, step)
        copies.append((
            pltpu.make_async_copy(error_ref.at[part], error_own.at[part], sems.at[1 + 2 * i]),
            pltpu.make_async_copy(grad_ref.at[part], grad_own.at[part], sems.at[2 + 2 * i]),
        ))
        for copy in copies[i]:
            copy.start()
    q_copy.wait()
    q = q_own[...]
    parts = []
    for i in range(CHUNKS):
        for copy in copies[i]:
            copy.wait()
        part = slice(i * step, (i + 1) * step)
        merged = grad_own[part].astype(F32) + error_own[part]
        high, low = split(merged)
        parts.append(dot(high, q, NT) + dot(low, q, NT))
    p = jnp.concatenate(parts, axis=0)
    half = rows // 2
    out_ref[...] = jnp.concatenate([p[:half], p[half:]], axis=1)


def arrange_kernel(grad_ref, error_ref, first_high_ref, first_low_ref, last_high_ref, last_low_ref):
    high, low = split(grad_ref[...].astype(F32) + error_ref[...])
    shape = (PARTS * SLOT, high.shape[1])
    row = lax.broadcasted_iota(jnp.int32, shape, 0)
    col = lax.broadcasted_iota(jnp.int32, shape, 1)
    within = row % SLOT
    place = OWN * (row // SLOT) + within
    first = (col == place).astype(F32).astype(BF16)
    last = ((col == place + SLOT) & (within < OWN - SLOT)).astype(F32).astype(BF16)
    first_high_ref[...] = dot(first, high, NT).astype(BF16)
    first_low_ref[...] = dot(first, low, NT).astype(BF16)
    last_high_ref[...] = dot(last, high, NT).astype(BF16)
    last_low_ref[...] = dot(last, low, NT).astype(BF16)


def sum_left_kernel(in_ref, out_ref):
    rows = in_ref.shape[0]
    total = jnp.sum(in_ref[...].reshape(rows // 8, 8, 128), axis=0)
    total = total + pltpu.roll(total, 4, 0)
    out_ref[...] = jnp.broadcast_to(total[None], (rows // 8, 8, 128)).reshape(rows, 128)


def right_kernel(p_ref, first_high_ref, first_low_ref, last_high_ref, last_low_ref, out_ref, gram_ref):
    top = p_ref[...]
    bottom = pltpu.roll(top, RANK, 1)
    lane = lax.broadcasted_iota(jnp.int32, top.shape, 1)
    lower = lane < RANK
    zero = jnp.zeros_like(top)
    left = jnp.concatenate([jnp.where(lower, top, zero), jnp.where(lower, bottom, zero)], axis=0)
    right = jnp.concatenate([jnp.where(lower, zero, bottom), jnp.where(lower, zero, top)], axis=0)
    left_high, left_low = split(left)
    right_high, right_low = split(right)
    left_both = jnp.concatenate([left_high, left_low], axis=1)
    right_both = jnp.concatenate([right_high, right_low], axis=1)
    both = (
        dot(first_high_ref[...], left_both, NN)
        + dot(last_high_ref[...], right_both, NN)
        + dot(first_low_ref[...], left_both, NN)
        + dot(last_low_ref[...], right_both, NN)
    )
    out_ref[...] = both[:, :128] + both[:, 128:]
    turned = top.T
    turned = jnp.concatenate([turned[:RANK], turned[RANK:]], axis=1)
    gram_ref[...] = dot3(turned, right, NN)
    for k in range(PARTS):
        out_ref[SLOT * k + 12 : SLOT * k + 14, RANK:] = gram_ref[2 * k : 2 * k + 2, RANK:]


def sum_right_kernel(in_ref, out_ref, own_ref):
    total = jnp.sum(in_ref[...].reshape(PARTS, SLOT, 128), axis=0)
    own_ref[...] = total
    out_ref[...] = jnp.broadcast_to(total[None], (PARTS, SLOT, 128)).reshape(PARTS * SLOT, 128)


def eliminate(tiles):
    sub = lax.broadcasted_iota(jnp.int32, (8, 128), 0)
    spread = lambda value: jnp.broadcast_to(value, (8, 128))
    at = lambda values, index: spread(values[index // 8][index % 8 : index % 8 + 1, :])
    scales = [jnp.zeros((8, 128), F32) for _ in tiles]
    count = len(tiles)
    for start in range(0, RANK, WIDTH):
        begin = start // 8
        cols = [
            {i: spread(tiles[i][:, RANK + start + q : RANK + start + q + 1]) for i in range(begin, count)}
            for q in range(WIDTH)
        ]
        rows = [at(tiles, start + q) for q in range(WIDTH)]
        for q in range(WIDTH):
            pivot_row = start + q
            t = pivot_row // 8
            pivot = at(cols[q], pivot_row)
            inverse = 1.0 / pivot
            root = lax.rsqrt(pivot)
            root = root * (1.5 - 0.5 * pivot * root * root)
            scales[t] = jnp.where(sub == pivot_row % 8, root, scales[t])
            scaled = rows[q] * inverse
            factor = {i: cols[q][i] for i in range(t, count)}
            factor[t] = jnp.where(sub > pivot_row % 8, cols[q][t], 0.0)
            for q2 in range(q + 1, WIDTH):
                entry = at(cols[q2], pivot_row) * inverse
                rows[q2] = rows[q2] - at(factor, start + q2) * scaled
                for i in range(t, count):
                    cols[q2][i] = cols[q2][i] - factor[i] * entry
            for i in range(t, count):
                tiles[i] = tiles[i] - factor[i] * scaled
    return [tile * scale for tile, scale in zip(tiles, scales)]


def error_kernel(grad_ref, error_ref, p_ref, s_ref, own_ref, error_out_ref, q_out_ref, table_ref, right_ref, result_ref, sems):
    rows, cols = error_ref.shape
    row = lax.broadcasted_iota(jnp.int32, (RANK, 128), 0)
    lane = lax.broadcasted_iota(jnp.int32, (RANK, 128), 1)
    table_ref[...] = (row == lane).astype(F32)
    for k in range(PARTS):
        table_ref[2 * k : 2 * k + 2, RANK:] = 0.5 * s_ref[SLOT * k + 12 : SLOT * k + 14, RANK:]
    tiles = eliminate([table_ref[8 * i : 8 * i + 8, :] for i in range(RANK // 8)])
    inverse = jnp.where(lane < RANK, jnp.concatenate(tiles, axis=0), 0.0)
    both = jnp.concatenate([inverse, pltpu.roll(inverse, RANK, 1)], axis=0)
    basis = dot3(p_ref[...], both, NT)
    turned = pltpu.roll(basis, RANK, 1)
    lower = lax.broadcasted_iota(jnp.int32, basis.shape, 1) < RANK
    whole = jnp.concatenate([jnp.where(lower, basis, turned), jnp.where(lower, turned, basis)], axis=0)
    high = whole.astype(BF16)
    low = jnp.where(jnp.concatenate([lower, lower], axis=0), whole - high.astype(F32), 0.0)
    left = jnp.concatenate([high, low.astype(BF16)], axis=0)
    right = 0.5 * dot3(s_ref[...], both, NT)
    high = right.astype(BF16).astype(F32)
    low = right - high
    lower = lax.broadcasted_iota(jnp.int32, right.shape, 1) < RANK
    first = jnp.where(lower, high, pltpu.roll(low, RANK, 1))
    last = jnp.where(lower, pltpu.roll(high, RANK, 1), low)
    for k in range(PARTS):
        right_ref[OWN * k : OWN * k + SLOT, :] = first[SLOT * k : SLOT * k + SLOT]
        right_ref[OWN * k + SLOT : OWN * k + OWN, :] = last[SLOT * k : SLOT * k + OWN - SLOT]
    copies = []
    for i in range(0, cols, 256):
        width = min(256, cols - i)
        products = dot(left, right_ref[i : i + width, :].astype(BF16), NT)
        merged = grad_ref[:, i : i + width].astype(F32) + error_ref[:, i : i + width]
        result_ref[:, i : i + width] = merged - (products[:rows] + products[rows:])
        part = pl.ds(i, width)
        copies.append(pltpu.make_async_copy(result_ref.at[:, part], error_out_ref.at[:, part], sems.at[i // 256]))
        copies[-1].start()
    own = 0.5 * dot3(own_ref[...], both, NT)
    q_out_ref[:SLOT, :] = own[:, :RANK]
    q_out_ref[SLOT:, :] = pltpu.roll(own, RANK, 1)[: OWN - SLOT, :RANK]
    for copy in copies:
        copy.wait()


def shape(*dims, kind=F32):
    return jax.ShapeDtypeStruct(dims, kind)


def params(limit=24):
    return pltpu.CompilerParams(vmem_limit_bytes=limit * 1024 * 1024)


def cost(flops, moved):
    return pl.CostEstimate(flops=flops, bytes_accessed=moved, transcendentals=0)


def shards(grad, error, q_start):
    rows, cols = grad.shape
    col = lax.axis_index("col").astype(jnp.int32).reshape(1)
    hbm = pl.BlockSpec(memory_space=pltpu.HBM)
    vmem = pl.BlockSpec(memory_space=pltpu.VMEM)
    smem = pl.BlockSpec(memory_space=pltpu.SMEM)
    with jax.named_scope("left"):
        p_own = pl.pallas_call(
            left_kernel,
            in_specs=[smem, hbm, hbm, hbm],
            out_specs=vmem,
            out_shape=shape(rows // 2, 128),
            scratch_shapes=[
                pltpu.VMEM((rows, cols), BF16),
                pltpu.VMEM((rows, cols), F32),
                pltpu.VMEM((RANK, cols), BF16),
                pltpu.SemaphoreType.DMA((1 + 2 * CHUNKS,)),
            ],
            compiler_params=params(LEFT_LIMIT),
        )(col, grad, error, q_start.T)
    with jax.named_scope("arrange"):
        p_own, grad, error = lax.optimization_barrier((p_own, grad, error))
        arranged = pl.pallas_call(
            arrange_kernel,
            out_shape=[shape(PARTS * SLOT, rows, kind=BF16)] * 4,
            compiler_params=params(),
            cost_estimate=cost(2 * 4 * 512 * 256 * 896, 2500000),
        )(grad, error)
    with jax.named_scope("left_scatter"):
        p_parts = lax.all_to_all(p_own, ("rep", "col"), 0, 0, tiled=True)
    with jax.named_scope("left_sum"):
        p_sum = pl.pallas_call(sum_left_kernel, out_shape=shape(rows // 2, 128), compiler_params=params())(p_parts)
    with jax.named_scope("left_gather"):
        p = lax.all_to_all(p_sum, ("rep", "col"), 0, 0, tiled=True)
    with jax.named_scope("right"):
        s_own = pl.pallas_call(
            right_kernel,
            out_shape=shape(PARTS * SLOT, 128),
            scratch_shapes=[pltpu.VMEM((RANK, 128), F32)],
            compiler_params=params(),
        )(p, *arranged)
    with jax.named_scope("right_scatter"):
        s_parts = lax.all_to_all(s_own, ("rep", "tensor"), 0, 0, tiled=True)
    with jax.named_scope("right_sum"):
        s_sum, s_piece = pl.pallas_call(
            sum_right_kernel,
            out_shape=[shape(PARTS * SLOT, 128), shape(SLOT, 128)],
            compiler_params=params(),
        )(s_parts)
    with jax.named_scope("right_owner"):
        own = lax.ppermute(
            s_piece, ("rep", "col"), [(s, REPLICAS * (s % 16) + s // 16) for s in range(PARTS)]
        )
    with jax.named_scope("right_gather"):
        s = lax.all_to_all(s_sum, ("rep", "tensor"), 0, 0, tiled=True)
    with jax.named_scope("new_error"):
        return pl.pallas_call(
            error_kernel,
            out_specs=[hbm, vmem],
            out_shape=[shape(rows, cols), shape(OWN, RANK)],
            scratch_shapes=[
                pltpu.VMEM((RANK, 128), F32),
                pltpu.VMEM((cols, 128), F32),
                pltpu.VMEM((rows, cols), F32),
                pltpu.SemaphoreType.DMA((-(-cols // 256),)),
            ],
            compiler_params=params(),
        )(grad, error, p, s, own)


def solution(mesh):
    n_dp, n_tensor = mesh.devices.shape
    fine = Mesh(mesh.devices.reshape(REPLICAS, n_dp // REPLICAS, n_tensor), ("rep", "col", "tensor"))
    blocks = P("tensor", ("rep", "col"))
    return jax.shard_map(
        shards,
        mesh=fine,
        in_specs=(blocks, blocks, P()),
        out_specs=(blocks, P(("rep", "col", "tensor"), None)),
        check_vma=False,
    )
```

```python
import jax
import jax.numpy as jnp
from jax import lax
from jax.experimental import pallas as pl
from jax.experimental.pallas import tpu as pltpu
from jax.sharding import Mesh, PartitionSpec as P

REPLICAS = 2
RANK = 64
PARTS = 32
OWN = 28
CORES = 2
HALF = PARTS // CORES
CHUNKS = 2
LEFT_LIMIT = 54912
PAYLOAD = 256
WIDTH = 8
SLOT = 16
NT = (((1,), (1,)), ((), ()))
NN = (((1,), (0,)), ((), ()))
BF16 = jnp.bfloat16
F32 = jnp.float32


def split(value):
    high = value.astype(BF16)
    return high, (value - high.astype(F32)).astype(BF16)


def dot(a, b, dims):
    return lax.dot_general(a, b, dims, preferred_element_type=F32)


def dot3(a, b, dims):
    a_high, a_low = split(a)
    b_high, b_low = split(b)
    return dot(a_high, b_high, dims) + (dot(a_high, b_low, dims) + dot(a_low, b_high, dims))


def left_kernel(col_ref, grad_ref, error_ref, q_ref, out_ref, grad_own, error_own, q_own, sems):
    rows, cols = grad_own.shape
    step = rows // CHUNKS
    start = pl.multiple_of(col_ref[0] * cols, 128)
    q_copy = pltpu.make_async_copy(q_ref.at[:, pl.ds(start, cols)], q_own, sems.at[0])
    q_copy.start()
    copies = []
    for i in range(CHUNKS):
        part = pl.ds(i * step, step)
        copies.append((
            pltpu.make_async_copy(error_ref.at[part], error_own.at[part], sems.at[1 + 2 * i]),
            pltpu.make_async_copy(grad_ref.at[part], grad_own.at[part], sems.at[2 + 2 * i]),
        ))
        for copy in copies[i]:
            copy.start()
    q_copy.wait()
    q = q_own[...]
    parts = []
    for i in range(CHUNKS):
        for copy in copies[i]:
            copy.wait()
        part = slice(i * step, (i + 1) * step)
        merged = grad_own[part].astype(F32) + error_own[part]
        high, low = split(merged)
        parts.append(dot(high, q, NT) + dot(low, q, NT))
    p = jnp.concatenate(parts, axis=0)
    half = rows // 2
    out_ref[...] = jnp.concatenate([p[:half], p[half:]], axis=1)


def arrange_kernel(grad_ref, error_ref, first_high_ref, first_low_ref, last_high_ref, last_low_ref):
    high, low = split(grad_ref[...].astype(F32) + error_ref[...])
    shape = (PARTS * SLOT, high.shape[1])
    row = lax.broadcasted_iota(jnp.int32, shape, 0)
    col = lax.broadcasted_iota(jnp.int32, shape, 1)
    within = row % SLOT
    place = OWN * (row // SLOT) + within
    first = (col == place).astype(F32).astype(BF16)
    last = ((col == place + SLOT) & (within < OWN - SLOT)).astype(F32).astype(BF16)
    first_high_ref[...] = dot(first, high, NT).astype(BF16)
    first_low_ref[...] = dot(first, low, NT).astype(BF16)
    last_high_ref[...] = dot(last, high, NT).astype(BF16)
    last_low_ref[...] = dot(last, low, NT).astype(BF16)


def sum_left_kernel(in_ref, out_ref):
    rows = in_ref.shape[0]
    total = jnp.sum(in_ref[...].reshape(rows // 8, 8, 128), axis=0)
    total = total + pltpu.roll(total, 4, 0)
    out_ref[...] = jnp.broadcast_to(total[None], (rows // 8, 8, 128)).reshape(rows, 128)


def right_kernel(p_ref, first_high_ref, first_low_ref, last_high_ref, last_low_ref, out_ref, gram_ref):
    top = p_ref[...]
    bottom = pltpu.roll(top, RANK, 1)
    lane = lax.broadcasted_iota(jnp.int32, top.shape, 1)
    lower = lane < RANK
    zero = jnp.zeros_like(top)
    left = jnp.concatenate([jnp.where(lower, top, zero), jnp.where(lower, bottom, zero)], axis=0)
    right = jnp.concatenate([jnp.where(lower, zero, bottom), jnp.where(lower, zero, top)], axis=0)
    left_high, left_low = split(left)
    right_high, right_low = split(right)
    left_both = jnp.concatenate([left_high, left_low], axis=1)
    right_both = jnp.concatenate([right_high, right_low], axis=1)
    both = (
        dot(first_high_ref[...], left_both, NN)
        + dot(last_high_ref[...], right_both, NN)
        + dot(first_low_ref[...], left_both, NN)
        + dot(last_low_ref[...], right_both, NN)
    )
    out_ref[...] = both[:, :128] + both[:, 128:]
    turned = top.T
    turned = jnp.concatenate([turned[:RANK], turned[RANK:]], axis=1)
    gram_ref[...] = dot3(turned, right, NN)
    for k in range(PARTS):
        first = 4 * (k // CORES)
        out_ref[SLOT * k + 12 : SLOT * k + 16, RANK:] = gram_ref[first : first + 4, RANK:]


def sum_right_kernel(in_ref, out_ref, own_ref):
    total = jnp.sum(in_ref[...].reshape(PARTS, SLOT, 128), axis=0)
    own_ref[...] = jnp.broadcast_to(total[None], (PAYLOAD // SLOT, SLOT, 128)).reshape(PAYLOAD, 128)
    out_ref[...] = jnp.broadcast_to(total[None], (HALF, SLOT, 128)).reshape(HALF * SLOT, 128)


def eliminate(tiles):
    sub = lax.broadcasted_iota(jnp.int32, (8, 128), 0)
    spread = lambda value: jnp.broadcast_to(value, (8, 128))
    at = lambda values, index: spread(values[index // 8][index % 8 : index % 8 + 1, :])
    scales = [jnp.zeros((8, 128), F32) for _ in tiles]
    count = len(tiles)
    for start in range(0, RANK, WIDTH):
        begin = start // 8
        cols = [
            {i: spread(tiles[i][:, RANK + start + q : RANK + start + q + 1]) for i in range(begin, count)}
            for q in range(WIDTH)
        ]
        rows = [at(tiles, start + q) for q in range(WIDTH)]
        for q in range(WIDTH):
            pivot_row = start + q
            t = pivot_row // 8
            pivot = at(cols[q], pivot_row)
            inverse = 1.0 / pivot
            root = lax.rsqrt(pivot)
            root = root * (1.5 - 0.5 * pivot * root * root)
            scales[t] = jnp.where(sub == pivot_row % 8, root, scales[t])
            scaled = rows[q] * inverse
            factor = {i: cols[q][i] for i in range(t, count)}
            factor[t] = jnp.where(sub > pivot_row % 8, cols[q][t], 0.0)
            for q2 in range(q + 1, WIDTH):
                entry = at(cols[q2], pivot_row) * inverse
                rows[q2] = rows[q2] - at(factor, start + q2) * scaled
                for i in range(t, count):
                    cols[q2][i] = cols[q2][i] - factor[i] * entry
            for i in range(t, count):
                tiles[i] = tiles[i] - factor[i] * scaled
    return [tile * scale for tile, scale in zip(tiles, scales)]


def basis_kernel(p_ref, s_ref, inverse_ref, basis_ref, table_ref):
    row = lax.broadcasted_iota(jnp.int32, (RANK, 128), 0)
    lane = lax.broadcasted_iota(jnp.int32, (RANK, 128), 1)
    table_ref[...] = (row == lane).astype(F32)
    for h in range(HALF):
        table_ref[4 * h : 4 * h + 4, RANK:] = 0.5 * s_ref[SLOT * h + 12 : SLOT * h + 16, RANK:]
    tiles = eliminate([table_ref[8 * i : 8 * i + 8, :] for i in range(RANK // 8)])
    inverse = jnp.where(lane < RANK, jnp.concatenate(tiles, axis=0), 0.0)
    turned = pltpu.roll(inverse, RANK, 1)
    high, low = split(inverse)
    inverse_ref[...] = jnp.concatenate([split(inverse + turned)[0], low], axis=0)
    basis = dot3(p_ref[...], jnp.concatenate([inverse, turned], axis=0), NT)
    turned = pltpu.roll(basis, RANK, 1)
    lower = lax.broadcasted_iota(jnp.int32, basis.shape, 1) < RANK
    whole = jnp.concatenate([jnp.where(lower, basis, turned), jnp.where(lower, turned, basis)], axis=0)
    high = whole.astype(BF16)
    low = jnp.where(jnp.concatenate([lower, lower], axis=0), whole - high.astype(F32), 0.0)
    basis_ref[...] = jnp.concatenate([high, low.astype(BF16)], axis=0)


def pair(s):
    lower = lax.broadcasted_iota(jnp.int32, s.shape, 1) < RANK
    high = s.astype(BF16).astype(F32)
    low = s - high
    return jnp.where(lower, high, pltpu.roll(low, RANK, 1)), jnp.where(lower, pltpu.roll(high, RANK, 1), low)


def error_kernel(core_ref, grad_ref, error_ref, inverse_ref, basis_ref, near_ref, far_ref, own_ref, error_out_ref, q_out_ref, right_ref, result_ref, own_out, sems):
    rows, cols = error_ref.shape
    inverse = inverse_ref[...]
    near = near_ref[...]
    far = far_ref[...]
    swapped = core_ref[0] == 1
    for core, s in enumerate((jnp.where(swapped, far, near), jnp.where(swapped, near, far))):
        first, last = pair(s)
        for h in range(HALF):
            start = OWN * (CORES * h + core)
            right_ref[start : start + SLOT, :] = first[SLOT * h : SLOT * h + SLOT]
            right_ref[start + SLOT : start + OWN, :] = last[SLOT * h : SLOT * h + OWN - SLOT]
    first, last = pair(own_ref[:SLOT])
    own = dot(jnp.concatenate([first, last], axis=0).astype(BF16), inverse, NT)
    own = 0.5 * (own + pltpu.roll(own, RANK, 1))
    own_out[...] = own[:OWN, :RANK]
    copies = [pltpu.make_async_copy(own_out, q_out_ref, sems.at[0])]
    copies[0].start()
    for i in range(0, cols, 256):
        width = min(256, cols - i)
        right = dot(inverse, right_ref[i : i + width, :].astype(BF16), NT)
        high, low = split(0.5 * (right[:RANK] + right[RANK:]))
        products = dot(basis_ref[...], jnp.concatenate([high, low], axis=0), NN)
        merged = grad_ref[:, i : i + width].astype(F32) + error_ref[:, i : i + width]
        result_ref[:, i : i + width] = merged - (products[:rows] + products[rows:])
        part = pl.ds(i, width)
        copies.append(pltpu.make_async_copy(result_ref.at[:, part], error_out_ref.at[:, part], sems.at[1 + i // 256]))
        copies[-1].start()
    for copy in copies:
        copy.wait()


def shape(*dims, kind=F32):
    return jax.ShapeDtypeStruct(dims, kind)


def params(limit=24 * 1024):
    return pltpu.CompilerParams(vmem_limit_bytes=limit * 1024)


def cost(flops, moved):
    return pl.CostEstimate(flops=flops, bytes_accessed=moved, transcendentals=0)


def shards(grad, error, q_start):
    rows, cols = grad.shape
    col = lax.axis_index("col").astype(jnp.int32).reshape(1)
    core = lax.axis_index("core").astype(jnp.int32).reshape(1)
    hbm = pl.BlockSpec(memory_space=pltpu.HBM)
    vmem = pl.BlockSpec(memory_space=pltpu.VMEM)
    smem = pl.BlockSpec(memory_space=pltpu.SMEM)
    with jax.named_scope("left"):
        p_own = pl.pallas_call(
            left_kernel,
            in_specs=[smem, hbm, hbm, hbm],
            out_specs=vmem,
            out_shape=shape(rows // 2, 128),
            scratch_shapes=[
                pltpu.VMEM((rows, cols), BF16),
                pltpu.VMEM((rows, cols), F32),
                pltpu.VMEM((RANK, cols), BF16),
                pltpu.SemaphoreType.DMA((1 + 2 * CHUNKS,)),
            ],
            compiler_params=params(LEFT_LIMIT),
        )(col, grad, error, q_start.T)
    with jax.named_scope("arrange"):
        p_own, grad, error = lax.optimization_barrier((p_own, grad, error))
        arranged = pl.pallas_call(
            arrange_kernel,
            out_shape=[shape(PARTS * SLOT, rows, kind=BF16)] * 4,
            compiler_params=params(),
            cost_estimate=cost(2 * 4 * 512 * 256 * 896, 2500000),
        )(grad, error)
    with jax.named_scope("left_scatter"):
        p_parts = lax.all_to_all(p_own, ("rep", "col"), 0, 0, tiled=True)
    with jax.named_scope("left_sum"):
        p_sum = pl.pallas_call(sum_left_kernel, out_shape=shape(rows // 2, 128), compiler_params=params())(p_parts)
    with jax.named_scope("left_gather"):
        p = lax.all_to_all(p_sum, ("rep", "col"), 0, 0, tiled=True)
    with jax.named_scope("right"):
        s_own = pl.pallas_call(
            right_kernel,
            out_shape=shape(PARTS * SLOT, 128),
            scratch_shapes=[pltpu.VMEM((RANK, 128), F32)],
            compiler_params=params(),
        )(p, *arranged)
    with jax.named_scope("right_scatter"):
        s_parts = lax.all_to_all(s_own, ("rep", "z", "core"), 0, 0, tiled=True)
    with jax.named_scope("right_sum"):
        s_sum, s_piece = pl.pallas_call(
            sum_right_kernel,
            out_shape=[shape(HALF * SLOT, 128), shape(PAYLOAD, 128)],
            compiler_params=params(),
        )(s_parts)
    with jax.named_scope("right_owner"):
        own = lax.ppermute(
            s_piece, ("rep", "col"), [(s, REPLICAS * (s % 16) + s // 16) for s in range(PARTS)]
        )
    with jax.named_scope("right_gather"):
        near = lax.all_to_all(s_sum, ("rep", "z"), 0, 0, tiled=True)
    with jax.named_scope("right_swap"):
        far = lax.ppermute(near, "core", [(0, 1), (1, 0)])
    with jax.named_scope("basis"):
        inverse, basis = pl.pallas_call(
            basis_kernel,
            out_shape=[shape(128, 128, kind=BF16), shape(2 * rows, 128, kind=BF16)],
            scratch_shapes=[pltpu.VMEM((RANK, 128), F32)],
            compiler_params=params(),
            cost_estimate=cost(1000, 1000),
        )(p, near)
    with jax.named_scope("new_error"):
        return pl.pallas_call(
            error_kernel,
            in_specs=[smem] + [vmem] * 7,
            out_specs=[hbm, hbm],
            out_shape=[shape(rows, cols), shape(OWN, RANK)],
            scratch_shapes=[
                pltpu.VMEM((cols, 128), F32),
                pltpu.VMEM((rows, cols), F32),
                pltpu.VMEM((OWN, RANK), F32),
                pltpu.SemaphoreType.DMA((1 + -(-cols // 256),)),
            ],
            compiler_params=params(),
            cost_estimate=cost(1000, 1000),
        )(core, grad, error, inverse, basis, near, far, own)


def solution(mesh):
    n_dp, n_tensor = mesh.devices.shape
    grid = mesh.devices.reshape(REPLICAS, n_dp // REPLICAS, n_tensor // CORES, CORES)
    fine = Mesh(grid, ("rep", "col", "z", "core"))
    blocks = P(("z", "core"), ("rep", "col"))
    return jax.shard_map(
        shards,
        mesh=fine,
        in_specs=(blocks, blocks, P()),
        out_specs=(blocks, P(("rep", "col", "z", "core"), None)),
        check_vma=False,
    )
```

```python
import jax
import jax.numpy as jnp
from jax import lax
from jax.experimental import pallas as pl
from jax.experimental.pallas import tpu as pltpu
from jax.sharding import Mesh, PartitionSpec as P

REPLICAS = 2
RANK = 64
PARTS = 32
OWN = 28
CORES = 2
HALF = PARTS // CORES
CHUNKS = 2
LEFT_LIMIT = 54912
PAYLOAD = 256
WIDTH = 8
SLOT = 16
NT = (((1,), (1,)), ((), ()))
NN = (((1,), (0,)), ((), ()))
BF16 = jnp.bfloat16
F32 = jnp.float32


def split(value):
    high = value.astype(BF16)
    return high, (value - high.astype(F32)).astype(BF16)


def dot(a, b, dims):
    return lax.dot_general(a, b, dims, preferred_element_type=F32)


def dot3(a, b, dims):
    a_high, a_low = split(a)
    b_high, b_low = split(b)
    return dot(a_high, b_high, dims) + (dot(a_high, b_low, dims) + dot(a_low, b_high, dims))


def left_kernel(col_ref, grad_ref, error_ref, q_ref, out_ref, grad_own, error_own, q_own, sems):
    rows, cols = grad_own.shape
    step = rows // CHUNKS
    start = pl.multiple_of(col_ref[0] * cols, 128)
    q_copy = pltpu.make_async_copy(q_ref.at[:, pl.ds(start, cols)], q_own, sems.at[0])
    q_copy.start()
    copies = []
    for i in range(CHUNKS):
        part = pl.ds(i * step, step)
        copies.append((
            pltpu.make_async_copy(error_ref.at[part], error_own.at[part], sems.at[1 + 2 * i]),
            pltpu.make_async_copy(grad_ref.at[part], grad_own.at[part], sems.at[2 + 2 * i]),
        ))
        for copy in copies[i]:
            copy.start()
    q_copy.wait()
    q = q_own[...]
    parts = []
    for i in range(CHUNKS):
        for copy in copies[i]:
            copy.wait()
        part = slice(i * step, (i + 1) * step)
        merged = grad_own[part].astype(F32) + error_own[part]
        high, low = split(merged)
        parts.append(dot(high, q, NT) + dot(low, q, NT))
    p = jnp.concatenate(parts, axis=0)
    half = rows // 2
    out_ref[...] = jnp.concatenate([p[:half], p[half:]], axis=1)


def arrange_kernel(core_ref, grad_ref, error_ref, first_high_ref, first_low_ref, last_high_ref, last_low_ref, other_ref):
    high, low = split(grad_ref[...].astype(F32) + error_ref[...])
    core = core_ref[0]
    shape = (HALF * SLOT, high.shape[1])
    row = lax.broadcasted_iota(jnp.int32, shape, 0)
    col = lax.broadcasted_iota(jnp.int32, shape, 1)
    within = row % SLOT
    offset = col - OWN * CORES * (row // SLOT) - within

    def pick(core):
        place = offset - OWN * core
        first = (place == 0).astype(F32).astype(BF16)
        last = ((place == SLOT) & (within < OWN - SLOT)).astype(F32).astype(BF16)
        return [dot(rows, part, NT) for rows in (first, last) for part in (high, low)]

    for ref, value in zip((first_high_ref, first_low_ref, last_high_ref, last_low_ref), pick(core)):
        ref[...] = value.astype(BF16)
    first_high, first_low, last_high, last_low = pick(1 - core)
    other_ref[: HALF * SLOT] = first_high + first_low
    other_ref[HALF * SLOT :] = last_high + last_low


def sum_left_kernel(in_ref, out_ref):
    rows = in_ref.shape[0]
    total = jnp.sum(in_ref[...].reshape(rows // 8, 8, 128), axis=0)
    total = total + pltpu.roll(total, 4, 0)
    for i in range(out_ref.shape[0] // 8):
        out_ref[8 * i : 8 * i + 8] = total


def spread_left(top):
    bottom = pltpu.roll(top, RANK, 1)
    lower = lax.broadcasted_iota(jnp.int32, top.shape, 1) < RANK
    zero = jnp.zeros_like(top)
    left = jnp.concatenate([jnp.where(lower, top, zero), jnp.where(lower, bottom, zero)], axis=0)
    right = jnp.concatenate([jnp.where(lower, zero, bottom), jnp.where(lower, zero, top)], axis=0)
    return left, right


def right_kernel(core_ref, parts_ref, first_high_ref, first_low_ref, last_high_ref, last_low_ref, other_ref, out_ref, p_ref, gram_ref):
    half = parts_ref.shape[0] // 2
    swapped = core_ref[0] == 1
    zero_p = parts_ref[:half]
    one_p = parts_ref[half:]
    near = jnp.where(swapped, one_p, zero_p)
    p_ref[...] = near
    first_high, first_low = split(other_ref[: HALF * SLOT])
    last_high, last_low = split(other_ref[HALF * SLOT :])
    blocks = (
        (near, first_high_ref[...], first_low_ref[...], last_high_ref[...], last_low_ref[...]),
        (jnp.where(swapped, zero_p, one_p), first_high, first_low, last_high, last_low),
    )
    both = None
    for p, first_high, first_low, last_high, last_low in blocks:
        left, right = spread_left(p)
        left_both = jnp.concatenate(split(left), axis=1)
        right_both = jnp.concatenate(split(right), axis=1)
        term = (
            dot(first_high, left_both, NN)
            + dot(last_high, right_both, NN)
            + dot(first_low, left_both, NN)
            + dot(last_low, right_both, NN)
        )
        both = term if both is None else both + term
    out_ref[...] = both[:, :128] + both[:, 128:]
    gram = None
    for p in (zero_p, one_p):
        turned = p.T
        turned = jnp.concatenate([turned[:RANK], turned[RANK:]], axis=1)
        term = dot3(turned, spread_left(p)[1], NN)
        gram = term if gram is None else gram + term
    gram_ref[...] = gram
    for h in range(HALF):
        out_ref[SLOT * h + 12 : SLOT * h + 16, RANK:] = gram_ref[4 * h : 4 * h + 4, RANK:]


def sum_right_kernel(in_ref, out_ref, own_ref):
    total = jnp.sum(in_ref[...].reshape(HALF, SLOT, 128), axis=0)
    own_ref[...] = jnp.broadcast_to(total[None], (PAYLOAD // SLOT, SLOT, 128)).reshape(PAYLOAD, 128)
    out_ref[...] = jnp.broadcast_to(total[None], (HALF, SLOT, 128)).reshape(HALF * SLOT, 128)


def eliminate(tiles):
    sub = lax.broadcasted_iota(jnp.int32, (8, 128), 0)
    spread = lambda value: jnp.broadcast_to(value, (8, 128))
    at = lambda values, index: spread(values[index // 8][index % 8 : index % 8 + 1, :])
    scales = [jnp.zeros((8, 128), F32) for _ in tiles]
    count = len(tiles)
    for start in range(0, RANK, WIDTH):
        begin = start // 8
        cols = [
            {i: spread(tiles[i][:, RANK + start + q : RANK + start + q + 1]) for i in range(begin, count)}
            for q in range(WIDTH)
        ]
        rows = [at(tiles, start + q) for q in range(WIDTH)]
        for q in range(WIDTH):
            pivot_row = start + q
            t = pivot_row // 8
            pivot = at(cols[q], pivot_row)
            inverse = 1.0 / pivot
            root = lax.rsqrt(pivot)
            root = root * (1.5 - 0.5 * pivot * root * root)
            scales[t] = jnp.where(sub == pivot_row % 8, root, scales[t])
            scaled = rows[q] * inverse
            factor = {i: cols[q][i] for i in range(t, count)}
            factor[t] = jnp.where(sub > pivot_row % 8, cols[q][t], 0.0)
            for q2 in range(q + 1, WIDTH):
                entry = at(cols[q2], pivot_row) * inverse
                rows[q2] = rows[q2] - at(factor, start + q2) * scaled
                for i in range(t, count):
                    cols[q2][i] = cols[q2][i] - factor[i] * entry
            for i in range(t, count):
                tiles[i] = tiles[i] - factor[i] * scaled
    return [tile * scale for tile, scale in zip(tiles, scales)]


def basis_kernel(p_ref, s_ref, inverse_ref, basis_ref, table_ref):
    row = lax.broadcasted_iota(jnp.int32, (RANK, 128), 0)
    lane = lax.broadcasted_iota(jnp.int32, (RANK, 128), 1)
    table_ref[...] = (row == lane).astype(F32)
    for h in range(HALF):
        table_ref[4 * h : 4 * h + 4, RANK:] = 0.5 * s_ref[SLOT * h + 12 : SLOT * h + 16, RANK:]
    tiles = eliminate([table_ref[8 * i : 8 * i + 8, :] for i in range(RANK // 8)])
    inverse = jnp.where(lane < RANK, jnp.concatenate(tiles, axis=0), 0.0)
    turned = pltpu.roll(inverse, RANK, 1)
    high, low = split(inverse)
    inverse_ref[...] = jnp.concatenate([split(inverse + turned)[0], low], axis=0)
    basis = dot3(p_ref[...], jnp.concatenate([inverse, turned], axis=0), NT)
    turned = pltpu.roll(basis, RANK, 1)
    lower = lax.broadcasted_iota(jnp.int32, basis.shape, 1) < RANK
    whole = jnp.concatenate([jnp.where(lower, basis, turned), jnp.where(lower, turned, basis)], axis=0)
    high = whole.astype(BF16)
    low = jnp.where(jnp.concatenate([lower, lower], axis=0), whole - high.astype(F32), 0.0)
    basis_ref[...] = jnp.concatenate([high, low.astype(BF16)], axis=0)


def pair(s):
    lower = lax.broadcasted_iota(jnp.int32, s.shape, 1) < RANK
    high = s.astype(BF16).astype(F32)
    low = s - high
    return jnp.where(lower, high, pltpu.roll(low, RANK, 1)), jnp.where(lower, pltpu.roll(high, RANK, 1), low)


def error_kernel(core_ref, grad_ref, error_ref, inverse_ref, basis_ref, near_ref, far_ref, own_ref, error_out_ref, q_out_ref, right_ref, result_ref, own_out, sems):
    rows, cols = error_ref.shape
    inverse = inverse_ref[...]
    near = near_ref[...]
    far = far_ref[...]
    swapped = core_ref[0] == 1
    for core, s in enumerate((jnp.where(swapped, far, near), jnp.where(swapped, near, far))):
        first, last = pair(s)
        for h in range(HALF):
            start = OWN * (CORES * h + core)
            right_ref[start : start + SLOT, :] = first[SLOT * h : SLOT * h + SLOT]
            right_ref[start + SLOT : start + OWN, :] = last[SLOT * h : SLOT * h + OWN - SLOT]
    first, last = pair(own_ref[:SLOT])
    own = dot(jnp.concatenate([first, last], axis=0).astype(BF16), inverse, NT)
    own = 0.5 * (own + pltpu.roll(own, RANK, 1))
    own_out[...] = own[:OWN, :RANK]
    copies = [pltpu.make_async_copy(own_out, q_out_ref, sems.at[0])]
    copies[0].start()
    for i in range(0, cols, 256):
        width = min(256, cols - i)
        right = dot(inverse, right_ref[i : i + width, :].astype(BF16), NT)
        high, low = split(0.5 * (right[:RANK] + right[RANK:]))
        products = dot(basis_ref[...], jnp.concatenate([high, low], axis=0), NN)
        merged = grad_ref[:, i : i + width].astype(F32) + error_ref[:, i : i + width]
        result_ref[:, i : i + width] = merged - (products[:rows] + products[rows:])
        part = pl.ds(i, width)
        copies.append(pltpu.make_async_copy(result_ref.at[:, part], error_out_ref.at[:, part], sems.at[1 + i // 256]))
        copies[-1].start()
    for copy in copies:
        copy.wait()


def shape(*dims, kind=F32):
    return jax.ShapeDtypeStruct(dims, kind)


def params(limit=24 * 1024):
    return pltpu.CompilerParams(vmem_limit_bytes=limit * 1024)


def cost(flops, moved):
    return pl.CostEstimate(flops=flops, bytes_accessed=moved, transcendentals=0)


def shards(grad, error, q_start):
    rows, cols = grad.shape
    col = lax.axis_index("col").astype(jnp.int32).reshape(1)
    core = lax.axis_index("core").astype(jnp.int32).reshape(1)
    hbm = pl.BlockSpec(memory_space=pltpu.HBM)
    vmem = pl.BlockSpec(memory_space=pltpu.VMEM)
    smem = pl.BlockSpec(memory_space=pltpu.SMEM)
    with jax.named_scope("left"):
        p_own = pl.pallas_call(
            left_kernel,
            in_specs=[smem, hbm, hbm, hbm],
            out_specs=vmem,
            out_shape=shape(rows // 2, 128),
            scratch_shapes=[
                pltpu.VMEM((rows, cols), BF16),
                pltpu.VMEM((rows, cols), F32),
                pltpu.VMEM((RANK, cols), BF16),
                pltpu.SemaphoreType.DMA((1 + 2 * CHUNKS,)),
            ],
            compiler_params=params(LEFT_LIMIT),
        )(col, grad, error, q_start.T)
    with jax.named_scope("arrange"):
        p_own, grad, error = lax.optimization_barrier((p_own, grad, error))
        *arranged, other = pl.pallas_call(
            arrange_kernel,
            in_specs=[smem, vmem, vmem],
            out_shape=[shape(HALF * SLOT, rows, kind=BF16)] * 4 + [shape(2 * HALF * SLOT, rows)],
            compiler_params=params(),
            cost_estimate=cost(2 * 4 * 512 * 256 * 896, 2500000),
        )(core, grad, error)
    with jax.named_scope("left_scatter"):
        p_parts = lax.all_to_all(p_own, ("rep", "col"), 0, 0, tiled=True)
    with jax.named_scope("left_sum"):
        p_sum = pl.pallas_call(sum_left_kernel, out_shape=shape(rows, 128), compiler_params=params())(p_parts)
    p_sum, other = lax.optimization_barrier((p_sum, other))
    with jax.named_scope("left_gather"):
        p_both = lax.all_to_all(p_sum, ("core", "rep", "col"), 0, 0, tiled=True)
    with jax.named_scope("exchange"):
        other = lax.ppermute(other, "core", [(0, 1), (1, 0)])
    with jax.named_scope("right"):
        s_own, p = pl.pallas_call(
            right_kernel,
            in_specs=[smem] + [vmem] * 6,
            out_shape=[shape(HALF * SLOT, 128), shape(rows // 2, 128)],
            scratch_shapes=[pltpu.VMEM((RANK, 128), F32)],
            compiler_params=params(),
        )(core, p_both, *arranged, other)
    with jax.named_scope("right_scatter"):
        s_parts = lax.all_to_all(s_own, ("rep", "z"), 0, 0, tiled=True)
    with jax.named_scope("right_sum"):
        s_sum, s_piece = pl.pallas_call(
            sum_right_kernel,
            out_shape=[shape(HALF * SLOT, 128), shape(PAYLOAD, 128)],
            compiler_params=params(),
        )(s_parts)
    with jax.named_scope("right_owner"):
        own = lax.ppermute(
            s_piece, ("rep", "col"), [(s, REPLICAS * (s % 16) + s // 16) for s in range(PARTS)]
        )
    with jax.named_scope("right_gather"):
        near = lax.all_to_all(s_sum, ("rep", "z"), 0, 0, tiled=True)
    with jax.named_scope("right_swap"):
        far = lax.ppermute(near, "core", [(0, 1), (1, 0)])
    with jax.named_scope("basis"):
        inverse, basis = pl.pallas_call(
            basis_kernel,
            out_shape=[shape(128, 128, kind=BF16), shape(2 * rows, 128, kind=BF16)],
            scratch_shapes=[pltpu.VMEM((RANK, 128), F32)],
            compiler_params=params(),
            cost_estimate=cost(1000, 1000),
        )(p, near)
    with jax.named_scope("new_error"):
        return pl.pallas_call(
            error_kernel,
            in_specs=[smem] + [vmem] * 7,
            out_specs=[hbm, hbm],
            out_shape=[shape(rows, cols), shape(OWN, RANK)],
            scratch_shapes=[
                pltpu.VMEM((cols, 128), F32),
                pltpu.VMEM((rows, cols), F32),
                pltpu.VMEM((OWN, RANK), F32),
                pltpu.SemaphoreType.DMA((1 + -(-cols // 256),)),
            ],
            compiler_params=params(),
            cost_estimate=cost(1000, 1000),
        )(core, grad, error, inverse, basis, near, far, own)


def solution(mesh):
    n_dp, n_tensor = mesh.devices.shape
    grid = mesh.devices.reshape(REPLICAS, n_dp // REPLICAS, n_tensor // CORES, CORES)
    fine = Mesh(grid, ("rep", "col", "z", "core"))
    blocks = P(("z", "core"), ("rep", "col"))
    return jax.shard_map(
        shards,
        mesh=fine,
        in_specs=(blocks, blocks, P()),
        out_specs=(blocks, P(("rep", "col", "z", "core"), None)),
        check_vma=False,
    )
```

```python
import jax
import jax.numpy as jnp
from jax import lax
from jax.experimental import pallas as pl
from jax.experimental.pallas import tpu as pltpu
from jax.sharding import Mesh, PartitionSpec as P

REPLICAS = 2
RANK = 64
PARTS = 32
OWN = 28
CORES = 2
HALF = PARTS // CORES
CHUNKS = 2
SENDS = (320, 128)
LEFT_LIMIT = 54912
PAYLOAD = 256
WIDTH = 8
SLOT = 16
TAIL = 12
NT = (((1,), (1,)), ((), ()))
NN = (((1,), (0,)), ((), ()))
BF16 = jnp.bfloat16
F32 = jnp.float32


def split(value):
    high = value.astype(BF16)
    return high, (value - high.astype(F32)).astype(BF16)


def dot(a, b, dims):
    return lax.dot_general(a, b, dims, preferred_element_type=F32)


def dot3(a, b, dims):
    a_high, a_low = split(a)
    b_high, b_low = split(b)
    return dot(a_high, b_high, dims) + (dot(a_high, b_low, dims) + dot(a_low, b_high, dims))


def left_kernel(col_ref, grad_ref, error_ref, q_ref, out_ref, grad_own, error_own, q_own, sems):
    rows, cols = grad_own.shape
    step = rows // CHUNKS
    start = pl.multiple_of(col_ref[0] * cols, 128)
    q_copy = pltpu.make_async_copy(q_ref.at[:, pl.ds(start, cols)], q_own, sems.at[0])
    q_copy.start()
    copies = []
    for i in range(CHUNKS):
        part = pl.ds(i * step, step)
        copies.append((
            pltpu.make_async_copy(error_ref.at[part], error_own.at[part], sems.at[1 + 2 * i]),
            pltpu.make_async_copy(grad_ref.at[part], grad_own.at[part], sems.at[2 + 2 * i]),
        ))
        for copy in copies[i]:
            copy.start()
    q_copy.wait()
    q = q_own[...]
    parts = []
    for i in range(CHUNKS):
        for copy in copies[i]:
            copy.wait()
        part = slice(i * step, (i + 1) * step)
        merged = grad_own[part].astype(F32) + error_own[part]
        high, low = split(merged)
        parts.append(dot(high, q, NT) + dot(low, q, NT))
    p = jnp.concatenate(parts, axis=0)
    half = rows // 2
    out_ref[...] = jnp.concatenate([p[:half], p[half:]], axis=1)


def arrange_kernel(core_ref, grad_ref, error_ref, first_high_ref, first_low_ref, last_high_ref, last_low_ref, *other_refs):
    high, low = split(grad_ref[...].astype(F32) + error_ref[...])
    core = core_ref[0]
    shape = (HALF * SLOT, high.shape[1])
    row = lax.broadcasted_iota(jnp.int32, shape, 0)
    col = lax.broadcasted_iota(jnp.int32, shape, 1)
    within = row % SLOT
    offset = col - OWN * CORES * (row // SLOT) - within

    def pick(core):
        place = offset - OWN * core
        first = (place == 0).astype(F32).astype(BF16)
        last = ((place == SLOT) & (within < OWN - SLOT)).astype(F32).astype(BF16)
        return [dot(rows, part, NT) for rows in (first, last) for part in (high, low)]

    for ref, value in zip((first_high_ref, first_low_ref, last_high_ref, last_low_ref), pick(core)):
        ref[...] = value.astype(BF16)
    shape = (HALF * TAIL, high.shape[1])
    row = lax.broadcasted_iota(jnp.int32, shape, 0)
    col = lax.broadcasted_iota(jnp.int32, shape, 1)
    place = OWN * (CORES * (row // TAIL) + 1 - core) + SLOT + row % TAIL
    tail = (col == place).astype(F32).astype(BF16)
    first_high, first_low = pick(1 - core)[:2]
    other = jnp.concatenate([first_high + first_low, dot(tail, high, NT) + dot(tail, low, NT)], axis=0)
    start = 0
    for size, ref in zip(SENDS, other_refs):
        ref[...] = other[start : start + size]
        start += size


def sum_left_kernel(in_ref, out_ref):
    rows = in_ref.shape[0]
    total = jnp.sum(in_ref[...].reshape(rows // 8, 8, 128), axis=0)
    total = total + pltpu.roll(total, 4, 0)
    for i in range(out_ref.shape[0] // 8):
        out_ref[8 * i : 8 * i + 8] = total


def spread_left(top):
    bottom = pltpu.roll(top, RANK, 1)
    lower = lax.broadcasted_iota(jnp.int32, top.shape, 1) < RANK
    zero = jnp.zeros_like(top)
    left = jnp.concatenate([jnp.where(lower, top, zero), jnp.where(lower, bottom, zero)], axis=0)
    right = jnp.concatenate([jnp.where(lower, zero, bottom), jnp.where(lower, zero, top)], axis=0)
    return left, right


def right_kernel(core_ref, parts_ref, first_high_ref, first_low_ref, last_high_ref, last_low_ref, *refs):
    *other_refs, out_ref, p_ref, gram_ref = refs
    half = parts_ref.shape[0] // 2
    swapped = core_ref[0] == 1
    zero_p = parts_ref[:half]
    one_p = parts_ref[half:]
    near = jnp.where(swapped, one_p, zero_p)
    p_ref[...] = near
    other = jnp.concatenate([ref[...] for ref in other_refs], axis=0)
    first_high, first_low = split(other[: HALF * SLOT])
    last_high, last_low = split(other[HALF * SLOT :])
    left, right = spread_left(near)
    left = jnp.concatenate(split(left), axis=1)
    right = jnp.concatenate(split(right), axis=1)
    both = (
        dot(first_high_ref[...], left, NN)
        + dot(last_high_ref[...], right, NN)
        + dot(first_low_ref[...], left, NN)
        + dot(last_low_ref[...], right, NN)
    )
    left, right = spread_left(jnp.where(swapped, zero_p, one_p))
    left = jnp.concatenate(split(left), axis=1)
    right = jnp.concatenate(split(right), axis=1)
    both = both + dot(first_high, left, NN) + dot(first_low, left, NN)
    tail = dot(last_high, right, NN) + dot(last_low, right, NN)
    out_ref[...] = both[:, :128] + both[:, 128:]
    tail = tail[:, :128] + tail[:, 128:]
    for h in range(HALF):
        part = slice(SLOT * h, SLOT * h + TAIL)
        out_ref[part, :] = out_ref[part, :] + tail[TAIL * h : TAIL * h + TAIL]
    gram = None
    for p in (zero_p, one_p):
        turned = p.T
        turned = jnp.concatenate([turned[:RANK], turned[RANK:]], axis=1)
        term = dot3(turned, spread_left(p)[1], NN)
        gram = term if gram is None else gram + term
    gram_ref[...] = gram
    for h in range(HALF):
        out_ref[SLOT * h + 12 : SLOT * h + 16, RANK:] = gram_ref[4 * h : 4 * h + 4, RANK:]


def sum_right_kernel(in_ref, out_ref, own_ref):
    total = jnp.sum(in_ref[...].reshape(HALF, SLOT, 128), axis=0)
    own_ref[...] = jnp.broadcast_to(total[None], (PAYLOAD // SLOT, SLOT, 128)).reshape(PAYLOAD, 128)
    out_ref[...] = jnp.broadcast_to(total[None], (HALF, SLOT, 128)).reshape(HALF * SLOT, 128)


def eliminate(tiles):
    sub = lax.broadcasted_iota(jnp.int32, (8, 128), 0)
    spread = lambda value: jnp.broadcast_to(value, (8, 128))
    at = lambda values, index: spread(values[index // 8][index % 8 : index % 8 + 1, :])
    scales = [jnp.zeros((8, 128), F32) for _ in tiles]
    count = len(tiles)
    for start in range(0, RANK, WIDTH):
        begin = start // 8
        cols = [
            {i: spread(tiles[i][:, RANK + start + q : RANK + start + q + 1]) for i in range(begin, count)}
            for q in range(WIDTH)
        ]
        rows = [at(tiles, start + q) for q in range(WIDTH)]
        for q in range(WIDTH):
            pivot_row = start + q
            t = pivot_row // 8
            pivot = at(cols[q], pivot_row)
            inverse = 1.0 / pivot
            root = lax.rsqrt(pivot)
            root = root * (1.5 - 0.5 * pivot * root * root)
            scales[t] = jnp.where(sub == pivot_row % 8, root, scales[t])
            scaled = rows[q] * inverse
            factor = {i: cols[q][i] for i in range(t, count)}
            factor[t] = jnp.where(sub > pivot_row % 8, cols[q][t], 0.0)
            for q2 in range(q + 1, WIDTH):
                entry = at(cols[q2], pivot_row) * inverse
                rows[q2] = rows[q2] - at(factor, start + q2) * scaled
                for i in range(t, count):
                    cols[q2][i] = cols[q2][i] - factor[i] * entry
            for i in range(t, count):
                tiles[i] = tiles[i] - factor[i] * scaled
    return [tile * scale for tile, scale in zip(tiles, scales)]


def basis_kernel(p_ref, s_ref, inverse_ref, basis_ref, table_ref):
    row = lax.broadcasted_iota(jnp.int32, (RANK, 128), 0)
    lane = lax.broadcasted_iota(jnp.int32, (RANK, 128), 1)
    table_ref[...] = (row == lane).astype(F32)
    for h in range(HALF):
        table_ref[4 * h : 4 * h + 4, RANK:] = 0.5 * s_ref[SLOT * h + 12 : SLOT * h + 16, RANK:]
    tiles = eliminate([table_ref[8 * i : 8 * i + 8, :] for i in range(RANK // 8)])
    inverse = jnp.where(lane < RANK, jnp.concatenate(tiles, axis=0), 0.0)
    turned = pltpu.roll(inverse, RANK, 1)
    high, low = split(inverse)
    inverse_ref[...] = jnp.concatenate([split(inverse + turned)[0], low], axis=0)
    basis = dot3(p_ref[...], jnp.concatenate([inverse, turned], axis=0), NT)
    turned = pltpu.roll(basis, RANK, 1)
    lower = lax.broadcasted_iota(jnp.int32, basis.shape, 1) < RANK
    whole = jnp.concatenate([jnp.where(lower, basis, turned), jnp.where(lower, turned, basis)], axis=0)
    high = whole.astype(BF16)
    low = jnp.where(jnp.concatenate([lower, lower], axis=0), whole - high.astype(F32), 0.0)
    basis_ref[...] = jnp.concatenate([high, low.astype(BF16)], axis=0)


def pair(s):
    lower = lax.broadcasted_iota(jnp.int32, s.shape, 1) < RANK
    high = s.astype(BF16).astype(F32)
    low = s - high
    return jnp.where(lower, high, pltpu.roll(low, RANK, 1)), jnp.where(lower, pltpu.roll(high, RANK, 1), low)


def error_kernel(core_ref, grad_ref, error_ref, inverse_ref, basis_ref, near_ref, far_ref, own_ref, error_out_ref, q_out_ref, right_ref, result_ref, own_out, sems):
    rows, cols = error_ref.shape
    inverse = inverse_ref[...]
    near = near_ref[...]
    far = far_ref[...]
    swapped = core_ref[0] == 1
    for core, s in enumerate((jnp.where(swapped, far, near), jnp.where(swapped, near, far))):
        first, last = pair(s)
        for h in range(HALF):
            start = OWN * (CORES * h + core)
            right_ref[start : start + SLOT, :] = first[SLOT * h : SLOT * h + SLOT]
            right_ref[start + SLOT : start + OWN, :] = last[SLOT * h : SLOT * h + OWN - SLOT]
    first, last = pair(own_ref[:SLOT])
    own = dot(jnp.concatenate([first, last], axis=0).astype(BF16), inverse, NT)
    own = 0.5 * (own + pltpu.roll(own, RANK, 1))
    own_out[...] = own[:OWN, :RANK]
    copies = [pltpu.make_async_copy(own_out, q_out_ref, sems.at[0])]
    copies[0].start()
    for i in range(0, cols, 256):
        width = min(256, cols - i)
        right = dot(inverse, right_ref[i : i + width, :].astype(BF16), NT)
        high, low = split(0.5 * (right[:RANK] + right[RANK:]))
        products = dot(basis_ref[...], jnp.concatenate([high, low], axis=0), NN)
        merged = grad_ref[:, i : i + width].astype(F32) + error_ref[:, i : i + width]
        result_ref[:, i : i + width] = merged - (products[:rows] + products[rows:])
        part = pl.ds(i, width)
        copies.append(pltpu.make_async_copy(result_ref.at[:, part], error_out_ref.at[:, part], sems.at[1 + i // 256]))
        copies[-1].start()
    for copy in copies:
        copy.wait()


def shape(*dims, kind=F32):
    return jax.ShapeDtypeStruct(dims, kind)


def params(limit=24 * 1024):
    return pltpu.CompilerParams(vmem_limit_bytes=limit * 1024)


def cost(flops, moved):
    return pl.CostEstimate(flops=flops, bytes_accessed=moved, transcendentals=0)


def shards(grad, error, q_start):
    rows, cols = grad.shape
    col = lax.axis_index("col").astype(jnp.int32).reshape(1)
    core = lax.axis_index("core").astype(jnp.int32).reshape(1)
    hbm = pl.BlockSpec(memory_space=pltpu.HBM)
    vmem = pl.BlockSpec(memory_space=pltpu.VMEM)
    smem = pl.BlockSpec(memory_space=pltpu.SMEM)
    with jax.named_scope("left"):
        p_own = pl.pallas_call(
            left_kernel,
            in_specs=[smem, hbm, hbm, hbm],
            out_specs=vmem,
            out_shape=shape(rows // 2, 128),
            scratch_shapes=[
                pltpu.VMEM((rows, cols), BF16),
                pltpu.VMEM((rows, cols), F32),
                pltpu.VMEM((RANK, cols), BF16),
                pltpu.SemaphoreType.DMA((1 + 2 * CHUNKS,)),
            ],
            compiler_params=params(LEFT_LIMIT),
        )(col, grad, error, q_start.T)
    with jax.named_scope("arrange"):
        p_own, grad, error = lax.optimization_barrier((p_own, grad, error))
        arranged = pl.pallas_call(
            arrange_kernel,
            in_specs=[smem, vmem, vmem],
            out_shape=[shape(HALF * SLOT, rows, kind=BF16)] * 4 + [shape(size, rows) for size in SENDS],
            compiler_params=params(),
            cost_estimate=cost(2 * 4 * 512 * 256 * 896, 2500000),
        )(core, grad, error)
    with jax.named_scope("left_scatter"):
        p_parts = lax.all_to_all(p_own, ("rep", "col"), 0, 0, tiled=True)
    with jax.named_scope("left_sum"):
        p_sum = pl.pallas_call(sum_left_kernel, out_shape=shape(rows, 128), compiler_params=params())(p_parts)
    p_sum, late = lax.optimization_barrier((p_sum, arranged[5:]))
    with jax.named_scope("left_gather"):
        p_both = lax.all_to_all(p_sum, ("core", "rep", "col"), 0, 0, tiled=True)
    with jax.named_scope("exchange"):
        other = [lax.ppermute(part, "core", [(0, 1), (1, 0)]) for part in [*arranged[4:5], *late]]
    with jax.named_scope("right"):
        s_own, p = pl.pallas_call(
            right_kernel,
            in_specs=[smem] + [vmem] * (5 + len(SENDS)),
            out_shape=[shape(HALF * SLOT, 128), shape(rows // 2, 128)],
            scratch_shapes=[pltpu.VMEM((RANK, 128), F32)],
            compiler_params=params(),
        )(core, p_both, *arranged[:4], *other)
    with jax.named_scope("right_scatter"):
        s_parts = lax.all_to_all(s_own, ("rep", "z"), 0, 0, tiled=True)
    with jax.named_scope("right_sum"):
        s_sum, s_piece = pl.pallas_call(
            sum_right_kernel,
            out_shape=[shape(HALF * SLOT, 128), shape(PAYLOAD, 128)],
            compiler_params=params(),
        )(s_parts)
    with jax.named_scope("right_owner"):
        own = lax.ppermute(
            s_piece, ("rep", "col"), [(s, REPLICAS * (s % 16) + s // 16) for s in range(PARTS)]
        )
    with jax.named_scope("right_gather"):
        near = lax.all_to_all(s_sum, ("rep", "z"), 0, 0, tiled=True)
    with jax.named_scope("right_swap"):
        far = lax.ppermute(near, "core", [(0, 1), (1, 0)])
    with jax.named_scope("basis"):
        inverse, basis = pl.pallas_call(
            basis_kernel,
            out_shape=[shape(128, 128, kind=BF16), shape(2 * rows, 128, kind=BF16)],
            scratch_shapes=[pltpu.VMEM((RANK, 128), F32)],
            compiler_params=params(),
            cost_estimate=cost(1000, 1000),
        )(p, near)
    with jax.named_scope("new_error"):
        return pl.pallas_call(
            error_kernel,
            in_specs=[smem] + [vmem] * 7,
            out_specs=[hbm, hbm],
            out_shape=[shape(rows, cols), shape(OWN, RANK)],
            scratch_shapes=[
                pltpu.VMEM((cols, 128), F32),
                pltpu.VMEM((rows, cols), F32),
                pltpu.VMEM((OWN, RANK), F32),
                pltpu.SemaphoreType.DMA((1 + -(-cols // 256),)),
            ],
            compiler_params=params(),
            cost_estimate=cost(1000, 1000),
        )(core, grad, error, inverse, basis, near, far, own)


def solution(mesh):
    n_dp, n_tensor = mesh.devices.shape
    grid = mesh.devices.reshape(REPLICAS, n_dp // REPLICAS, n_tensor // CORES, CORES)
    fine = Mesh(grid, ("rep", "col", "z", "core"))
    blocks = P(("z", "core"), ("rep", "col"))
    return jax.shard_map(
        shards,
        mesh=fine,
        in_specs=(blocks, blocks, P()),
        out_specs=(blocks, P(("rep", "col", "z", "core"), None)),
        check_vma=False,
    )
```
